32 devices in a mesh: region: 4 (over z), sub: 8 (over y, x, core).
Axes of the slice: x: 2, y: 2, z: 4, core: 2. Of those that a mesh axis runs over, the one named last changes fastest.
Arguments:
- members: bfloat16 [1024, 65536], P(('region', 'sub'))
- obs_perturb: bfloat16 [8192, 1024], P(('region', 'sub')), may hold values from -6 to 6
- innovations: bfloat16 [8192], P(('region', 'sub')), may hold values from -12 to 12
- obs_list: int32 [32, 2048], P(('region', 'sub')), may hold values from 0 to 2047, as said below
- obs_blocks: int32 [32], P(('region', 'sub')), may hold values from 8 to 16, as said below
- obs_precision: float32 [32, 2048], P(('region', 'sub')), may hold values from 0.1 to 1
- interp_slots: int32 [2048, 2], P(('region', 'sub')), may hold values from 0 to 2, as said below
- interp_weight: float32 [2048], P(('region', 'sub')), may hold values from 0.2 to 0.8
Outputs:
- analysis: bfloat16 [1024, 65536], P(None, ('region', 'sub'))
The draws below stay inside these ranges and needn't reach their ends.
Inputs may be any that keep to these rules, and one draw needn't show every extreme that they name: `obs_list`: the 2048 entries of a point's list are distinct. Entries from obs_blocks * 128 on are padding; some point uses all 2048 entries. `interp_slots`: the two slots of a column differ.
All inputs are finite; a program needn't handle non-finite values.
Results may differ from the reference program's by a relative error of at most 0.0058.
Values may be sent and summed in bfloat16 or wider, within the bound.
A program may use at most 128 MiB of HBM per device.

```python
import math
import jax
import jax.numpy as jnp
from jax import lax

K = 1024
LEV = 8
VARS = 4
COL_DEV = 64
LMAX = 2048
BLOCK = 128
ITERS = 2
NPTS = 32
NCOL = 2048
GROUP_ROWS = 2048
NOBS = 8192
N_REGION = 4
N_SUB = 8


def draw_members(key, part):
    key = jax.random.fold_in(key, 11)
    key_mean, key_scale, key_pert = jax.random.split(key, 3)
    width = NCOL * LEV * VARS
    mean_field = 1.5 * jax.random.normal(key_mean, (1, width), jnp.float32)
    spread = jnp.exp(jax.random.uniform(key_scale, (1, width), jnp.float32, jnp.log(0.3), jnp.log(3.0)))
    pert = jax.random.normal(key_pert, (K, width), jnp.float32)
    return (mean_field + spread * pert).astype(jnp.bfloat16)


def draw_obs_list(key, part):
    key = jax.random.fold_in(key, 23)
    keys = jax.random.split(key, NPTS)

    def one_list(single):
        return jax.random.permutation(single, GROUP_ROWS)[:LMAX].astype(jnp.int32)
    return jax.vmap(one_list)(keys)


def draw_obs_blocks(key, part):
    key = jax.random.fold_in(key, 37)
    key_count, key_place = jax.random.split(key)
    counts = jax.random.randint(key_count, (NPTS,), LMAX // BLOCK // 2, LMAX // BLOCK + 1).astype(jnp.int32)
    place = jax.random.randint(key_place, (), 0, NPTS)
    return counts.at[place].set(LMAX // BLOCK)


def draw_interp_slots(key, part):
    key = jax.random.fold_in(key, 41)
    key_first, key_step = jax.random.split(key)
    first = jax.random.randint(key_first, (NCOL,), 0, 3).astype(jnp.int32)
    second = (first + jax.random.randint(key_step, (NCOL,), 1, 3).astype(jnp.int32)) % 3
    return jnp.stack([first, second], axis=1).astype(jnp.int32)


def levels(key, extent, shards, least, largest):
    def one(position, shards_of):
        draws = jax.random.uniform(jax.random.fold_in(jax.random.fold_in(key, 6), position), (shards_of,), jnp.float32, least / len(shards), largest / len(shards))
        return jnp.repeat(jnp.exp(draws), extent[position] // shards_of).reshape((-1,) + (1,) * (len(extent) - position - 1))

    gain = one(*shards[0])
    for cut in shards[1:]:
        gain = gain * one(*cut)
    return gain


def bell_draw(stream_key, dims, scale, limit, pieces=(), kind=jnp.bfloat16):
    factor_of = levels(stream_key, dims, pieces, -0.22, 0.18) if pieces else 1.0
    drawn = jax.random.normal(stream_key, dims, jnp.float32) * scale * factor_of
    return jnp.minimum(jnp.maximum(drawn, -limit), limit).astype(kind)


def setup_inputs(seed: int = 0) -> dict:
    key_of = jax.random.split(jax.random.key(seed), 9)
    members = draw_members(jax.random.fold_in(key_of[8], 71), 0)
    obs_perturb = bell_draw(key_of[1], (NOBS, K), 1.0, 6.0, ((0, 32),))
    innovations = bell_draw(key_of[2], (NOBS,), 2.0, 12.0, ((0, 32),))
    obs_list = draw_obs_list(jax.random.fold_in(key_of[8], 71), 0)
    obs_blocks = draw_obs_blocks(jax.random.fold_in(key_of[8], 71), 0)
    obs_precision = jnp.clip(jnp.exp(math.log(1.0) - 2.3025851 * jax.random.uniform(key_of[5], (NPTS, LMAX), jnp.float32) ** levels(key_of[5], (NPTS, LMAX), ((0, 32),), -0.2, 0.2)), 0.1, 1.0)
    interp_slots = draw_interp_slots(jax.random.fold_in(key_of[8], 71), 0)
    interp_weight = jnp.clip(0.2 + 0.6 * jax.random.uniform(key_of[7], (NCOL,), jnp.float32) ** levels(key_of[7], (NCOL,), ((0, 32),), -0.2, 0.2), 0.2, 0.8)
    return dict(members=members, obs_perturb=obs_perturb, innovations=innovations, obs_list=obs_list, obs_blocks=obs_blocks, obs_precision=obs_precision, interp_slots=interp_slots, interp_weight=interp_weight)


def exact_dot(left, right):
    return jnp.dot(left, right, precision=lax.Precision.HIGHEST)

def finish_weights(gram_sum, drive_vec):
    size_k = gram_sum.shape[0]
    identity = jnp.eye(size_k, dtype=jnp.float32)
    system = identity + gram_sum / (size_k - 1)
    norm_scale = 2.0 * jnp.sqrt(jnp.sum(system * system) / size_k + 1e-06)
    scaled = system / norm_scale
    factor = 0.5 * (3.0 * identity - scaled)
    sqrt_iter = exact_dot(scaled, factor)
    inv_iter = factor
    for turn_index in range(ITERS - 1):
        factor = 0.5 * (3.0 * identity - exact_dot(inv_iter, sqrt_iter))
        if turn_index + 2 < ITERS:
            sqrt_iter = exact_dot(sqrt_iter, factor)
        inv_iter = exact_dot(factor, inv_iter)
    root_weight = inv_iter / jnp.sqrt(norm_scale)
    mean_weight = exact_dot(root_weight, exact_dot(root_weight, drive_vec)) / (size_k - 1)
    return (root_weight + mean_weight[:, None]).astype(jnp.bfloat16)

def contract_rows(left, right):
    return lax.dot_general(left, right, (((0,), (0,)), ((), ())), preferred_element_type=jnp.float32)

def reference(members, obs_perturb, innovations, obs_list, obs_blocks, obs_precision, interp_slots, interp_weight):
    group_rows = obs_perturb.reshape(N_REGION, GROUP_ROWS, K)
    group_innov = innovations.reshape(N_REGION, GROUP_ROWS)
    points = jnp.arange(NPTS, dtype=jnp.int32)

    def point_weights(inputs):
        point, list_rows, block_count, precision = inputs
        region_index = point // N_SUB
        local_rows = jnp.take(group_rows[region_index], list_rows, axis=0)
        local_innov = jnp.take(group_innov[region_index], list_rows).astype(jnp.float32)
        inside = jnp.arange(LMAX, dtype=jnp.int32) < block_count * BLOCK
        row_weight = jnp.where(inside, precision, jnp.float32(0.0))
        weighted = (local_rows.astype(jnp.float32) * row_weight[:, None]).astype(jnp.bfloat16)
        gram_sum = contract_rows(local_rows, weighted)
        drive_vec = exact_dot(local_innov, weighted.astype(jnp.float32))
        return finish_weights(gram_sum, drive_vec)
    weights = lax.map(point_weights, (points, obs_list, obs_blocks, obs_precision))
    width = COL_DEV * LEV * VARS
    slot_table = interp_slots.reshape(NPTS, COL_DEV, 2)
    share_table = interp_weight.reshape(NPTS, COL_DEV)

    def point_update(inputs):
        point, slot_pair, coef = inputs
        block_data = lax.dynamic_slice_in_dim(members, point * width, width, 1)
        mean_field = lax.optimization_barrier(jnp.sum(block_data, axis=0, dtype=jnp.float32)) / K
        anomaly = (block_data.astype(jnp.float32) - mean_field).astype(jnp.bfloat16)
        region_index = point // N_SUB
        sub_index = point % N_SUB
        total = jnp.broadcast_to(mean_field, block_data.shape)
        for slot in range(3):
            neighbour = region_index * N_SUB + (sub_index + slot - 1 + N_SUB) % N_SUB
            share = jnp.where(slot_pair[:, 0] == slot, coef, jnp.float32(0.0)) + jnp.where(slot_pair[:, 1] == slot, 1.0 - coef, jnp.float32(0.0))
            share_row = jnp.repeat(share, LEV * VARS)
            total = total + share_row * contract_rows(weights[neighbour], anomaly)
        return total.astype(jnp.bfloat16)
    blocks_out = lax.map(point_update, (points, slot_table, share_table))
    return blocks_out.transpose(1, 0, 2).reshape(K, NPTS * width)
```

```python
import jax
import jax.numpy as jnp
from jax import lax
from jax.experimental import pallas as pl
from jax.experimental.pallas import tpu as pltpu
from jax.sharding import PartitionSpec as P

LEV = 8
VARS = 4
BLOCK = 128
EXTRA = 16
TILE = 256
VMEM_BYTES = 60 * 1024 * 1024
POLY = (1.38671875, -1.140625, 0.9375, -0.4375, 0.0625)


def rows_weight(list_rows, rho, group_rows):
    rows = lax.broadcasted_iota(jnp.int32, (group_rows, list_rows.shape[0]), 0)
    return jnp.sum(jnp.where(rows == list_rows[None, :], rho[None, :], 0.0), axis=1)


def weights_kernel(obs_ref, row_ref, extra_ref, out_ref, flat, turned, left, held, cb, xb, wb, drive):
    blocks, _, size_k = obs_ref.shape
    dev_rows = flat.shape[0] // blocks
    tiles = size_k // TILE

    @pl.when(pl.program_id(0) == 0)
    def _():
        @pl.loop(0, blocks)
        def _(i):
            part = obs_ref[i, :dev_rows, :]
            at = pl.ds(pl.multiple_of(i * dev_rows, dev_rows), dev_rows)
            flat[at, :] = part
            turned[:, at] = part.T

    @pl.loop(0, blocks)
    def _(i):
        at = pl.ds(pl.multiple_of(i * dev_rows, dev_rows), dev_rows)
        left[:size_k, at] = (turned[:, at].astype(jnp.float32) * row_ref[0, :, at]).astype(jnp.bfloat16)

    left[size_k:, :] = extra_ref[0]

    def columns(c):
        return pl.ds(pl.multiple_of(c * TILE, TILE), TILE)

    def diagonal(c):
        row = lax.broadcasted_iota(jnp.int32, (size_k, TILE), 0)
        col = lax.broadcasted_iota(jnp.int32, (size_k, TILE), 1) + c * TILE
        return row == col

    def gram_tile(c, square):
        at = columns(c)
        both = jnp.dot(left[...], flat[:, at], preferred_element_type=jnp.float32)
        system = jnp.where(diagonal(c), 1.0, 0.0) + both[:size_k] * (1.0 / (size_k - 1))
        held[:, at] = system
        drive[0:1, at] = both[size_k : size_k + 1] + both[size_k + 1 : size_k + 2]
        return square + jnp.sum(system * system, axis=0, keepdims=True)

    square = lax.fori_loop(0, tiles, gram_tile, jnp.zeros((1, TILE), jnp.float32))
    total = jnp.sum(square, axis=1, keepdims=True)
    norm_scale = 2.0 * jnp.sqrt(total / size_k + 1e-06)
    inv_norm = 1.0 / norm_scale
    inv_root = 1.0 / jnp.sqrt(norm_scale)

    @pl.loop(0, tiles)
    def _(c):
        at = columns(c)
        centred = held[:, at] * inv_norm - jnp.where(diagonal(c), 0.5, 0.0)
        held[:, at] = centred
        cb[:, at] = centred.astype(jnp.bfloat16)

    @pl.loop(0, tiles)
    def _(c):
        at = columns(c)
        second = jnp.dot(cb[...], cb[:, at], preferred_element_type=jnp.float32)
        first = held[:, at]
        xb[:, at] = second.astype(jnp.bfloat16)
        wb[:, at] = (POLY[4] * second + POLY[3] * first).astype(jnp.bfloat16)
        held[:, at] = jnp.where(diagonal(c), POLY[0], 0.0) + POLY[1] * first + POLY[2] * second

    def root_tile(c, acc):
        at = columns(c)
        high = jnp.dot(xb[...], wb[:, at], preferred_element_type=jnp.float32)
        root = (held[:, at] + high) * inv_root
        held[:, at] = root
        return acc + jnp.sum(root * drive[0:1, at], axis=1, keepdims=True)

    inner = lax.fori_loop(0, tiles, root_tile, jnp.zeros((size_k, 1), jnp.float32))

    @pl.loop(0, tiles)
    def _(c):
        at = columns(c)
        root = held[:, at]
        mean_weight = jnp.sum(root * inner, axis=0, keepdims=True) * (1.0 / (size_k - 1))
        out_ref[0, :, at] = (root + mean_weight).astype(jnp.bfloat16)


def three_weights(gathered, row_weight, extra, dev_rows):
    blocks, aug_rows, size_k = gathered.shape
    rows = blocks * dev_rows
    flops = 3 * 2 * size_k * size_k * (rows + 2 * size_k)
    return pl.pallas_call(
        weights_kernel,
        grid=(3,),
        out_shape=jax.ShapeDtypeStruct((3, size_k, size_k), jnp.bfloat16),
        in_specs=[
            pl.BlockSpec((blocks, aug_rows, size_k), lambda t: (0, 0, 0), pipeline_mode=pl.Buffered(1)),
            pl.BlockSpec((1, 1, rows), lambda t: (t, 0, 0)),
            pl.BlockSpec((1, EXTRA, rows), lambda t: (t, 0, 0)),
        ],
        out_specs=pl.BlockSpec((1, size_k, size_k), lambda t: (t, 0, 0)),
        scratch_shapes=[
            pltpu.VMEM((rows, size_k), jnp.bfloat16),
            pltpu.VMEM((size_k, rows), jnp.bfloat16),
            pltpu.VMEM((size_k + EXTRA, rows), jnp.bfloat16),
            pltpu.VMEM((size_k, size_k), jnp.float32),
            pltpu.VMEM((size_k, size_k), jnp.bfloat16),
            pltpu.VMEM((size_k, size_k), jnp.bfloat16),
            pltpu.VMEM((size_k, size_k), jnp.bfloat16),
            pltpu.VMEM((8, size_k), jnp.float32),
        ],
        compiler_params=pltpu.CompilerParams(vmem_limit_bytes=VMEM_BYTES),
        cost_estimate=pl.CostEstimate(flops=flops, bytes_accessed=12 * 1024 * 1024, transcendentals=0),
    )(gathered, row_weight, extra)


def blend_kernel(member_ref, weight_ref, share_ref, out_ref):
    values = member_ref[...].astype(jnp.float32)
    mean_field = jnp.sum(values, axis=0, keepdims=True) / values.shape[0]
    anomaly = (values - mean_field).astype(jnp.bfloat16)
    total = mean_field
    for t in range(3):
        moved = jnp.dot(weight_ref[t], anomaly, preferred_element_type=jnp.float32)
        total = total + share_ref[t : t + 1, :] * moved
    out_ref[...] = total.astype(jnp.bfloat16)


def blend(by_column, weights, shares):
    size_k, width = by_column.shape
    return pl.pallas_call(
        blend_kernel,
        grid=(width // TILE,),
        out_shape=jax.ShapeDtypeStruct(by_column.shape, jnp.bfloat16),
        in_specs=[
            pl.BlockSpec((size_k, TILE), lambda c: (0, c)),
            pl.BlockSpec(weights.shape, lambda c: (0, 0, 0), pipeline_mode=pl.Buffered(1)),
            pl.BlockSpec((3, TILE), lambda c: (0, c)),
        ],
        out_specs=pl.BlockSpec((size_k, TILE), lambda c: (0, c)),
        compiler_params=pltpu.CompilerParams(vmem_limit_bytes=VMEM_BYTES),
        cost_estimate=pl.CostEstimate(
            flops=6 * size_k * size_k * width, bytes_accessed=14 * 1024 * 1024, transcendentals=0
        ),
    )(by_column, weights, shares)


def split(values):
    high = lax.reduce_precision(values, 8, 7)
    low = lax.reduce_precision(values - high, 8, 7)
    return high.astype(jnp.bfloat16), low.astype(jnp.bfloat16)


def gather_rows(packed):
    return lax.all_gather(packed, "sub", axis=0)


def local(
    members,
    obs_perturb,
    innovations,
    obs_list,
    obs_blocks,
    obs_precision,
    interp_slots,
    interp_weight,
):
    n_sub = lax.axis_size("sub")
    me = lax.axis_index("sub")
    dev_rows, size_k = obs_perturb.shape
    rows = n_sub * dev_rows
    inside = jnp.arange(obs_list.shape[1], dtype=jnp.int32) < obs_blocks[0] * BLOCK
    rho = jnp.where(inside, obs_precision[0], jnp.float32(0.0))
    high, low = split(rows_weight(obs_list[0], rho, rows))
    tail = jnp.concatenate([high, low, innovations])
    tail = jnp.pad(tail, (0, EXTRA * size_k - tail.shape[0])).reshape(EXTRA, size_k)
    gathered = gather_rows(jnp.concatenate([obs_perturb, tail], axis=0))
    by_column = lax.all_to_all(members, ("region", "sub"), split_axis=1, concat_axis=0, tiled=True)

    tails = gathered[:, dev_rows:, :].reshape(n_sub, EXTRA * size_k)
    innov = tails[:, 2 * rows : 2 * rows + dev_rows].reshape(rows).astype(jnp.float32)
    near = jnp.stack(
        [lax.dynamic_index_in_dim(tails, lax.rem(me + s, n_sub), 0, False) for s in (n_sub - 1, 0, 1)]
    ).astype(jnp.float32)
    weight = near[:, :rows] + near[:, rows : 2 * rows]
    extra = jnp.stack(split(weight * innov[None, :]), axis=1)
    extra = jnp.pad(extra, ((0, 0), (0, EXTRA - 2), (0, 0)))
    weights = three_weights(gathered, weight[:, None, :], extra, dev_rows)

    slots = jnp.arange(3, dtype=jnp.int32)[:, None]
    share = jnp.where(interp_slots[None, :, 0] == slots, interp_weight[None], 0.0) + jnp.where(
        interp_slots[None, :, 1] == slots, 1.0 - interp_weight[None], 0.0
    )
    return blend(by_column, weights, jnp.repeat(share, LEV * VARS, axis=1))


def solution(mesh):
    in_specs = (
        P(("region", "sub"), None),
        P(("region", "sub"), None),
        P(("region", "sub")),
        P(("region", "sub"), None),
        P(("region", "sub")),
        P(("region", "sub"), None),
        P(("region", "sub"), None),
        P(("region", "sub")),
    )
    out_specs = P(None, ("region", "sub"))
    return jax.shard_map(local, mesh=mesh, in_specs=in_specs, out_specs=out_specs, check_vma=False)
```

```python
import functools

import jax
import jax.numpy as jnp
from jax import lax
from jax.experimental import pallas as pl
from jax.experimental.pallas import tpu as pltpu
from jax.sharding import PartitionSpec as P

LEV = 8
VARS = 4
BLOCK = 128
EXTRA = 16
TILE = 256
VMEM_BYTES = 60 * 1024 * 1024
POLY = (1.38671875, -1.140625, 0.9375, -0.4375, 0.0625)


def rows_weight(list_rows, rho, group_rows):
    rows = lax.broadcasted_iota(jnp.int32, (group_rows, list_rows.shape[0]), 0)
    return jnp.sum(jnp.where(rows == list_rows[None, :], rho[None, :], 0.0), axis=1)


def weights_kernel(obs_ref, row_ref, extra_ref, out_ref, sum_ref, flat, turned, left, held, cb, xb, wb, drive):
    blocks, _, size_k = obs_ref.shape
    dev_rows = flat.shape[0] // blocks
    tiles = size_k // TILE

    @pl.when(pl.program_id(0) == 0)
    def _():
        @pl.loop(0, blocks)
        def _(i):
            part = obs_ref[i, :dev_rows, :]
            at = pl.ds(pl.multiple_of(i * dev_rows, dev_rows), dev_rows)
            flat[at, :] = part
            turned[:, at] = part.T

    @pl.loop(0, blocks)
    def _(i):
        at = pl.ds(pl.multiple_of(i * dev_rows, dev_rows), dev_rows)
        left[:size_k, at] = (turned[:, at].astype(jnp.float32) * row_ref[0, :, at]).astype(jnp.bfloat16)

    left[size_k:, :] = extra_ref[0]

    def columns(c):
        return pl.ds(pl.multiple_of(c * TILE, TILE), TILE)

    def diagonal(c):
        row = lax.broadcasted_iota(jnp.int32, (size_k, TILE), 0)
        col = lax.broadcasted_iota(jnp.int32, (size_k, TILE), 1) + c * TILE
        return row == col

    def gram_tile(c, square):
        at = columns(c)
        both = jnp.dot(left[...], flat[:, at], preferred_element_type=jnp.float32)
        system = jnp.where(diagonal(c), 1.0, 0.0) + both[:size_k] * (1.0 / (size_k - 1))
        held[:, at] = system
        drive[0:1, at] = both[size_k : size_k + 1] + both[size_k + 1 : size_k + 2]
        return square + jnp.sum(system * system, axis=0, keepdims=True)

    square = lax.fori_loop(0, tiles, gram_tile, jnp.zeros((1, TILE), jnp.float32))
    total = jnp.sum(square, axis=1, keepdims=True)
    norm_scale = 2.0 * jnp.sqrt(total / size_k + 1e-06)
    inv_norm = 1.0 / norm_scale
    inv_root = 1.0 / jnp.sqrt(norm_scale)

    @pl.loop(0, tiles)
    def _(c):
        at = columns(c)
        centred = held[:, at] * inv_norm - jnp.where(diagonal(c), 0.5, 0.0)
        held[:, at] = centred
        cb[:, at] = centred.astype(jnp.bfloat16)

    @pl.loop(0, tiles)
    def _(c):
        at = columns(c)
        second = jnp.dot(cb[...], cb[:, at], preferred_element_type=jnp.float32)
        first = held[:, at]
        xb[:, at] = second.astype(jnp.bfloat16)
        wb[:, at] = (POLY[4] * second + POLY[3] * first).astype(jnp.bfloat16)
        held[:, at] = jnp.where(diagonal(c), POLY[0], 0.0) + POLY[1] * first + POLY[2] * second

    def root_tile(c, acc):
        at = columns(c)
        high = jnp.dot(xb[...], wb[:, at], preferred_element_type=jnp.float32)
        root = (held[:, at] + high) * inv_root
        held[:, at] = root
        return acc + jnp.sum(root * drive[0:1, at], axis=1, keepdims=True)

    inner = lax.fori_loop(0, tiles, root_tile, jnp.zeros((size_k, 1), jnp.float32))

    def final_tile(c, acc):
        at = columns(c)
        root = held[:, at]
        mean_weight = jnp.sum(root * inner, axis=0, keepdims=True) * (1.0 / (size_k - 1))
        rounded = (root + mean_weight).astype(jnp.bfloat16)
        out_ref[0, :, at] = rounded
        return acc + jnp.sum(rounded.astype(jnp.float32), axis=1, keepdims=True)

    sum_ref[0] = lax.fori_loop(0, tiles, final_tile, jnp.zeros((size_k, 1), jnp.float32))


def three_weights(gathered, row_weight, extra, dev_rows):
    blocks, aug_rows, size_k = gathered.shape
    rows = blocks * dev_rows
    flops = 3 * 2 * size_k * size_k * (rows + 2 * size_k)
    return pl.pallas_call(
        weights_kernel,
        grid=(3,),
        out_shape=(
            jax.ShapeDtypeStruct((3, size_k, size_k), jnp.bfloat16),
            jax.ShapeDtypeStruct((3, size_k, 1), jnp.float32),
        ),
        in_specs=[
            pl.BlockSpec((blocks, aug_rows, size_k), lambda t: (0, 0, 0), pipeline_mode=pl.Buffered(1)),
            pl.BlockSpec((1, 1, rows), lambda t: (t, 0, 0)),
            pl.BlockSpec((1, EXTRA, rows), lambda t: (t, 0, 0)),
        ],
        out_specs=(
            pl.BlockSpec((1, size_k, size_k), lambda t: (t, 0, 0)),
            pl.BlockSpec((1, size_k, 1), lambda t: (t, 0, 0)),
        ),
        scratch_shapes=[
            pltpu.VMEM((rows, size_k), jnp.bfloat16),
            pltpu.VMEM((size_k, rows), jnp.bfloat16),
            pltpu.VMEM((size_k + EXTRA, rows), jnp.bfloat16),
            pltpu.VMEM((size_k, size_k), jnp.float32),
            pltpu.VMEM((size_k, size_k), jnp.bfloat16),
            pltpu.VMEM((size_k, size_k), jnp.bfloat16),
            pltpu.VMEM((size_k, size_k), jnp.bfloat16),
            pltpu.VMEM((8, size_k), jnp.float32),
        ],
        compiler_params=pltpu.CompilerParams(vmem_limit_bytes=VMEM_BYTES),
        cost_estimate=pl.CostEstimate(flops=flops, bytes_accessed=12 * 1024 * 1024, transcendentals=0),
    )(gathered, row_weight, extra)


def blend_kernel(member_ref, weight_ref, sum_ref, share_ref, out_ref):
    values = member_ref[...]
    mean_field = jnp.sum(values.astype(jnp.float32), axis=0, keepdims=True) / values.shape[0]
    total = mean_field
    for t in range(3):
        moved = jnp.dot(weight_ref[t], values, preferred_element_type=jnp.float32)
        total = total + share_ref[t : t + 1, :] * (moved - sum_ref[t] * mean_field)
    out_ref[...] = total.astype(jnp.bfloat16)


def blend(by_column, weights, sums, shares):
    size_k, width = by_column.shape
    return pl.pallas_call(
        blend_kernel,
        grid=(width // TILE,),
        out_shape=jax.ShapeDtypeStruct(by_column.shape, jnp.bfloat16),
        in_specs=[
            pl.BlockSpec((size_k, TILE), lambda c: (0, c)),
            pl.BlockSpec(weights.shape, lambda c: (0, 0, 0), pipeline_mode=pl.Buffered(1)),
            pl.BlockSpec(sums.shape, lambda c: (0, 0, 0), pipeline_mode=pl.Buffered(1)),
            pl.BlockSpec((3, TILE), lambda c: (0, c)),
        ],
        out_specs=pl.BlockSpec((size_k, TILE), lambda c: (0, c)),
        compiler_params=pltpu.CompilerParams(vmem_limit_bytes=VMEM_BYTES),
        cost_estimate=pl.CostEstimate(
            flops=6 * size_k * size_k * width, bytes_accessed=14 * 1024 * 1024, transcendentals=0
        ),
    )(by_column, weights, sums, shares)


def split(values):
    high = lax.reduce_precision(values, 8, 7)
    low = lax.reduce_precision(values - high, 8, 7)
    return high.astype(jnp.bfloat16), low.astype(jnp.bfloat16)


def gather_kernel(half, src, dst, out_send, out_recv, pair_send, pair_recv, own):
    me = lax.axis_index("sub")
    core, chip = lax.rem(me, 2), me // 2
    partner = me + 1 - 2 * core

    def same(offset):
        return 2 * lax.rem(chip + offset, half) + core

    def remote(source, slot, send, recv, target):
        return pltpu.make_async_remote_copy(
            src_ref=source,
            dst_ref=dst.at[slot],
            send_sem=send,
            recv_sem=recv,
            device_id={"sub": target},
            device_id_type=pl.DeviceIdType.MESH,
        )

    barrier = pltpu.get_barrier_semaphore()
    for target in [partner] + [same(i) for i in range(1, half)]:
        pl.semaphore_signal(barrier, inc=1, device_id={"sub": target}, device_id_type=pl.DeviceIdType.MESH)
    pl.semaphore_wait(barrier, half)

    outward = []
    for i in range(1, half):
        outward.append(remote(src, me, out_send.at[i], out_recv.at[i], same(i)))
        outward[-1].start()
    across = [remote(src, me, pair_send.at[0], pair_recv.at[0], partner)]
    across[0].start()
    kept = pltpu.make_async_copy(src, dst.at[me], own)
    kept.start()
    for i in range(1, half):
        outward[i - 1].wait_recv()
        owner = same(half - i)
        across.append(remote(dst.at[owner], owner, pair_send.at[i], pair_recv.at[i], partner))
        across[-1].start()
    kept.wait()
    for copy in outward:
        copy.wait_send()
    for copy in across:
        copy.wait()


def gather_rows(packed):
    size = lax.axis_size("sub")
    half = size // 2
    return pl.pallas_call(
        functools.partial(gather_kernel, half),
        out_shape=jax.ShapeDtypeStruct((size,) + packed.shape, packed.dtype),
        in_specs=[pl.BlockSpec(memory_space=pl.ANY)],
        out_specs=pl.BlockSpec(memory_space=pl.ANY),
        scratch_shapes=[pltpu.SemaphoreType.DMA((half,))] * 4 + [pltpu.SemaphoreType.DMA],
        compiler_params=pltpu.CompilerParams(collective_id=0, has_side_effects=True),
        cost_estimate=pl.CostEstimate(flops=0, bytes_accessed=64 * 1024 * 1024, transcendentals=0),
    )(packed)


def local(
    members,
    obs_perturb,
    innovations,
    obs_list,
    obs_blocks,
    obs_precision,
    interp_slots,
    interp_weight,
):
    n_sub = lax.axis_size("sub")
    me = lax.axis_index("sub")
    dev_rows, size_k = obs_perturb.shape
    rows = n_sub * dev_rows
    inside = jnp.arange(obs_list.shape[1], dtype=jnp.int32) < obs_blocks[0] * BLOCK
    rho = jnp.where(inside, obs_precision[0], jnp.float32(0.0))
    high, low = split(rows_weight(obs_list[0], rho, rows))
    tail = jnp.concatenate([high, low, innovations])
    tail = jnp.pad(tail, (0, EXTRA * size_k - tail.shape[0])).reshape(EXTRA, size_k)
    gathered = gather_rows(jnp.concatenate([obs_perturb, tail], axis=0))
    by_column = lax.all_to_all(members, ("region", "sub"), split_axis=1, concat_axis=0, tiled=True)

    tails = gathered[:, dev_rows:, :].reshape(n_sub, EXTRA * size_k)
    innov = tails[:, 2 * rows : 2 * rows + dev_rows].reshape(rows).astype(jnp.float32)
    near = jnp.stack(
        [lax.dynamic_index_in_dim(tails, lax.rem(me + s, n_sub), 0, False) for s in (n_sub - 1, 0, 1)]
    ).astype(jnp.float32)
    weight = near[:, :rows] + near[:, rows : 2 * rows]
    extra = jnp.stack(split(weight * innov[None, :]), axis=1)
    extra = jnp.pad(extra, ((0, 0), (0, EXTRA - 2), (0, 0)))
    weights, sums = three_weights(gathered, weight[:, None, :], extra, dev_rows)

    slots = jnp.arange(3, dtype=jnp.int32)[:, None]
    share = jnp.where(interp_slots[None, :, 0] == slots, interp_weight[None], 0.0) + jnp.where(
        interp_slots[None, :, 1] == slots, 1.0 - interp_weight[None], 0.0
    )
    return blend(by_column, weights, sums, jnp.repeat(share, LEV * VARS, axis=1))


def solution(mesh):
    in_specs = (
        P(("region", "sub"), None),
        P(("region", "sub"), None),
        P(("region", "sub")),
        P(("region", "sub"), None),
        P(("region", "sub")),
        P(("region", "sub"), None),
        P(("region", "sub"), None),
        P(("region", "sub")),
    )
    out_specs = P(None, ("region", "sub"))
    return jax.shard_map(local, mesh=mesh, in_specs=in_specs, out_specs=out_specs, check_vma=False)
```

```python
import functools

import jax
import jax.numpy as jnp
from jax import lax
from jax.experimental import pallas as pl
from jax.experimental.pallas import tpu as pltpu
from jax.sharding import PartitionSpec as P

LEV = 8
VARS = 4
BLOCK = 128
EXTRA = 16
TILE = 256
BLEND_TILE = 512
VMEM_BYTES = 60 * 1024 * 1024
POLY = (1.38671875, -1.140625, 0.9375, -0.4375, 0.0625)


def rows_weight(list_rows, rho, group_rows):
    rows = lax.broadcasted_iota(jnp.int32, (group_rows, list_rows.shape[0]), 0)
    return jnp.sum(jnp.where(rows == list_rows[None, :], rho[None, :], 0.0), axis=1)


def weights_kernel(obs_ref, row_ref, extra_ref, out_ref, flat, turned, left, held, cb, xb, wb, drive):
    blocks, _, size_k = obs_ref.shape
    dev_rows = flat.shape[0] // blocks
    tiles = size_k // TILE

    @pl.when(pl.program_id(0) == 0)
    def _():
        @pl.loop(0, blocks)
        def _(i):
            part = obs_ref[i, :dev_rows, :]
            at = pl.ds(pl.multiple_of(i * dev_rows, dev_rows), dev_rows)
            flat[at, :] = part
            turned[:, at] = part.T

    @pl.loop(0, blocks)
    def _(i):
        at = pl.ds(pl.multiple_of(i * dev_rows, dev_rows), dev_rows)
        left[:size_k, at] = (turned[:, at].astype(jnp.float32) * row_ref[0, :, at]).astype(jnp.bfloat16)

    left[size_k:, :] = extra_ref[0]

    def columns(c):
        return pl.ds(pl.multiple_of(c * TILE, TILE), TILE)

    def diagonal(c):
        row = lax.broadcasted_iota(jnp.int32, (size_k, TILE), 0)
        col = lax.broadcasted_iota(jnp.int32, (size_k, TILE), 1) + c * TILE
        return row == col

    def gram_tile(c, square):
        at = columns(c)
        both = jnp.dot(left[...], flat[:, at], preferred_element_type=jnp.float32)
        system = jnp.where(diagonal(c), 1.0, 0.0) + both[:size_k] * (1.0 / (size_k - 1))
        held[:, at] = system
        drive[0:1, at] = both[size_k : size_k + 1] + both[size_k + 1 : size_k + 2]
        return square + jnp.sum(system * system, axis=0, keepdims=True)

    square = lax.fori_loop(0, tiles, gram_tile, jnp.zeros((1, TILE), jnp.float32))
    total = jnp.sum(square, axis=1, keepdims=True)
    norm_scale = 2.0 * jnp.sqrt(total / size_k + 1e-06)
    inv_norm = 1.0 / norm_scale
    inv_root = 1.0 / jnp.sqrt(norm_scale)

    @pl.loop(0, tiles)
    def _(c):
        at = columns(c)
        centred = held[:, at] * inv_norm - jnp.where(diagonal(c), 0.5, 0.0)
        held[:, at] = centred
        cb[:, at] = centred.astype(jnp.bfloat16)

    @pl.loop(0, tiles)
    def _(c):
        at = columns(c)
        second = jnp.dot(cb[...], cb[:, at], preferred_element_type=jnp.float32)
        first = held[:, at]
        xb[:, at] = second.astype(jnp.bfloat16)
        wb[:, at] = (POLY[4] * second + POLY[3] * first).astype(jnp.bfloat16)
        held[:, at] = jnp.where(diagonal(c), POLY[0], 0.0) + POLY[1] * first + POLY[2] * second

    def root_tile(c, acc):
        at = columns(c)
        high = jnp.dot(xb[...], wb[:, at], preferred_element_type=jnp.float32)
        root = (held[:, at] + high) * inv_root
        held[:, at] = root
        return acc + jnp.sum(root * drive[0:1, at], axis=1, keepdims=True)

    inner = lax.fori_loop(0, tiles, root_tile, jnp.zeros((size_k, 1), jnp.float32))

    @pl.loop(0, tiles)
    def _(c):
        at = columns(c)
        root = held[:, at]
        mean_weight = jnp.sum(root * inner, axis=0, keepdims=True) * (1.0 / (size_k - 1))
        out_ref[:, at] = (root + mean_weight).astype(jnp.bfloat16)


def three_weights(gathered, row_weight, extra, dev_rows):
    blocks, aug_rows, size_k = gathered.shape
    rows = blocks * dev_rows
    flops = 3 * 2 * size_k * size_k * (rows + 2 * size_k)
    return pl.pallas_call(
        weights_kernel,
        grid=(3,),
        out_shape=jax.ShapeDtypeStruct((size_k, 3 * size_k), jnp.bfloat16),
        in_specs=[
            pl.BlockSpec((blocks, aug_rows, size_k), lambda t: (0, 0, 0), pipeline_mode=pl.Buffered(1)),
            pl.BlockSpec((1, 1, rows), lambda t: (t, 0, 0)),
            pl.BlockSpec((1, EXTRA, rows), lambda t: (t, 0, 0)),
        ],
        out_specs=pl.BlockSpec((size_k, size_k), lambda t: (0, t)),
        scratch_shapes=[
            pltpu.VMEM((rows, size_k), jnp.bfloat16),
            pltpu.VMEM((size_k, rows), jnp.bfloat16),
            pltpu.VMEM((size_k + EXTRA, rows), jnp.bfloat16),
            pltpu.VMEM((size_k, size_k), jnp.float32),
            pltpu.VMEM((size_k, size_k), jnp.bfloat16),
            pltpu.VMEM((size_k, size_k), jnp.bfloat16),
            pltpu.VMEM((size_k, size_k), jnp.bfloat16),
            pltpu.VMEM((8, size_k), jnp.float32),
        ],
        compiler_params=pltpu.CompilerParams(vmem_limit_bytes=VMEM_BYTES),
        cost_estimate=pl.CostEstimate(flops=flops, bytes_accessed=12 * 1024 * 1024, transcendentals=0),
    )(gathered, row_weight, extra)


def blend_kernel(member_ref, weight_ref, share_ref, out_ref, shared):
    values = member_ref[...].astype(jnp.float32)
    size_k = values.shape[0]
    mean_field = jnp.sum(values, axis=0, keepdims=True) / size_k
    anomaly = values - mean_field
    for t in range(3):
        shared[t * size_k : (t + 1) * size_k, :] = (anomaly * share_ref[t : t + 1, :]).astype(jnp.bfloat16)
    moved = jnp.dot(weight_ref[...], shared[...], preferred_element_type=jnp.float32)
    out_ref[...] = (moved + mean_field).astype(jnp.bfloat16)


def blend(by_column, weights, shares):
    size_k, width = by_column.shape
    return pl.pallas_call(
        blend_kernel,
        grid=(width // BLEND_TILE,),
        out_shape=jax.ShapeDtypeStruct(by_column.shape, jnp.bfloat16),
        in_specs=[
            pl.BlockSpec((size_k, BLEND_TILE), lambda c: (0, c)),
            pl.BlockSpec(weights.shape, lambda c: (0, 0), pipeline_mode=pl.Buffered(1)),
            pl.BlockSpec((3, BLEND_TILE), lambda c: (0, c)),
        ],
        out_specs=pl.BlockSpec((size_k, BLEND_TILE), lambda c: (0, c)),
        scratch_shapes=[pltpu.VMEM((3 * size_k, BLEND_TILE), jnp.bfloat16)],
        compiler_params=pltpu.CompilerParams(vmem_limit_bytes=VMEM_BYTES),
        cost_estimate=pl.CostEstimate(
            flops=6 * size_k * size_k * width, bytes_accessed=14 * 1024 * 1024, transcendentals=0
        ),
    )(by_column, weights, shares)


def split(values):
    high = lax.reduce_precision(values, 8, 7)
    low = lax.reduce_precision(values - high, 8, 7)
    return high.astype(jnp.bfloat16), low.astype(jnp.bfloat16)


def gather_kernel(half, src, dst, out_send, out_recv, pair_send, pair_recv, own):
    me = lax.axis_index("sub")
    core, chip = lax.rem(me, 2), me // 2
    partner = me + 1 - 2 * core

    def same(offset):
        return 2 * lax.rem(chip + offset, half) + core

    def remote(source, slot, send, recv, target):
        return pltpu.make_async_remote_copy(
            src_ref=source,
            dst_ref=dst.at[slot],
            send_sem=send,
            recv_sem=recv,
            device_id={"sub": target},
            device_id_type=pl.DeviceIdType.MESH,
        )

    barrier = pltpu.get_barrier_semaphore()
    for target in [partner] + [same(i) for i in range(1, half)]:
        pl.semaphore_signal(barrier, inc=1, device_id={"sub": target}, device_id_type=pl.DeviceIdType.MESH)
    pl.semaphore_wait(barrier, half)

    outward = []
    for i in range(1, half):
        outward.append(remote(src, me, out_send.at[i], out_recv.at[i], same(i)))
        outward[-1].start()
    across = [remote(src, me, pair_send.at[0], pair_recv.at[0], partner)]
    across[0].start()
    kept = pltpu.make_async_copy(src, dst.at[me], own)
    kept.start()
    for i in range(1, half):
        outward[i - 1].wait_recv()
        owner = same(half - i)
        across.append(remote(dst.at[owner], owner, pair_send.at[i], pair_recv.at[i], partner))
        across[-1].start()
    kept.wait()
    for copy in outward:
        copy.wait_send()
    for copy in across:
        copy.wait()


def gather_rows(packed):
    size = lax.axis_size("sub")
    half = size // 2
    return pl.pallas_call(
        functools.partial(gather_kernel, half),
        out_shape=jax.ShapeDtypeStruct((size,) + packed.shape, packed.dtype),
        in_specs=[pl.BlockSpec(memory_space=pl.ANY)],
        out_specs=pl.BlockSpec(memory_space=pl.ANY),
        scratch_shapes=[pltpu.SemaphoreType.DMA((half,))] * 4 + [pltpu.SemaphoreType.DMA],
        compiler_params=pltpu.CompilerParams(collective_id=0, has_side_effects=True),
        cost_estimate=pl.CostEstimate(flops=0, bytes_accessed=64 * 1024 * 1024, transcendentals=0),
    )(packed)


def local(
    members,
    obs_perturb,
    innovations,
    obs_list,
    obs_blocks,
    obs_precision,
    interp_slots,
    interp_weight,
):
    n_sub = lax.axis_size("sub")
    me = lax.axis_index("sub")
    dev_rows, size_k = obs_perturb.shape
    rows = n_sub * dev_rows
    inside = jnp.arange(obs_list.shape[1], dtype=jnp.int32) < obs_blocks[0] * BLOCK
    rho = jnp.where(inside, obs_precision[0], jnp.float32(0.0))
    high, low = split(rows_weight(obs_list[0], rho, rows))
    tail = jnp.concatenate([high, low, innovations])
    tail = jnp.pad(tail, (0, EXTRA * size_k - tail.shape[0])).reshape(EXTRA, size_k)
    gathered = gather_rows(jnp.concatenate([obs_perturb, tail], axis=0))
    members, gathered = lax.optimization_barrier((members, gathered))
    by_column = lax.all_to_all(members, ("region", "sub"), split_axis=1, concat_axis=0, tiled=True)

    tails = gathered[:, dev_rows:, :].reshape(n_sub, EXTRA * size_k)
    innov = tails[:, 2 * rows : 2 * rows + dev_rows].reshape(rows).astype(jnp.float32)
    near = jnp.stack(
        [lax.dynamic_index_in_dim(tails, lax.rem(me + s, n_sub), 0, False) for s in (n_sub - 1, 0, 1)]
    ).astype(jnp.float32)
    weight = near[:, :rows] + near[:, rows : 2 * rows]
    extra = jnp.stack(split(weight * innov[None, :]), axis=1)
    extra = jnp.pad(extra, ((0, 0), (0, EXTRA - 2), (0, 0)))
    weights = three_weights(gathered, weight[:, None, :], extra, dev_rows)

    slots = jnp.arange(3, dtype=jnp.int32)[:, None]
    share = jnp.where(interp_slots[None, :, 0] == slots, interp_weight[None], 0.0) + jnp.where(
        interp_slots[None, :, 1] == slots, 1.0 - interp_weight[None], 0.0
    )
    return blend(by_column, weights, jnp.repeat(share, LEV * VARS, axis=1))


def solution(mesh):
    in_specs = (
        P(("region", "sub"), None),
        P(("region", "sub"), None),
        P(("region", "sub")),
        P(("region", "sub"), None),
        P(("region", "sub")),
        P(("region", "sub"), None),
        P(("region", "sub"), None),
        P(("region", "sub")),
    )
    out_specs = P(None, ("region", "sub"))
    return jax.shard_map(local, mesh=mesh, in_specs=in_specs, out_specs=out_specs, check_vma=False)
```

```python
import functools

import jax
import jax.numpy as jnp
from jax import lax
from jax.experimental import pallas as pl
from jax.experimental.pallas import tpu as pltpu
from jax.sharding import PartitionSpec as P

LEV = 8
VARS = 4
BLOCK = 128
EXTRA = 16
TILE = 512
BLEND_TILE = 512
VMEM_BYTES = 60 * 1024 * 1024
POLY = (1.38671875, -1.140625, 0.9375, -0.4375, 0.0625)


def rows_weight(list_rows, rho, group_rows):
    rows = lax.broadcasted_iota(jnp.int32, (group_rows, list_rows.shape[0]), 0)
    return jnp.sum(jnp.where(rows == list_rows[None, :], rho[None, :], 0.0), axis=1)


def weights_kernel(first_ref, second_ref, row_ref, extra_ref, out_ref, flat, turned, left, held, cb, xb, wb, drive):
    blocks, half_rows, size_k = first_ref.shape
    dev_rows = flat.shape[0] // blocks
    tiles = size_k // TILE

    @pl.when(pl.program_id(0) == 0)
    def _():
        @pl.loop(0, blocks)
        def _(i):
            for j, ref in enumerate((first_ref, second_ref)):
                part = ref[i, :half_rows, :]
                at = pl.ds(pl.multiple_of(i * dev_rows + j * half_rows, half_rows), half_rows)
                flat[at, :] = part
                turned[:, at] = part.T

    @pl.loop(0, blocks)
    def _(i):
        at = pl.ds(pl.multiple_of(i * dev_rows, dev_rows), dev_rows)
        left[:size_k, at] = (turned[:, at].astype(jnp.float32) * row_ref[0, :, at]).astype(jnp.bfloat16)

    left[size_k:, :] = extra_ref[0]

    def columns(c):
        return pl.ds(pl.multiple_of(c * TILE, TILE), TILE)

    def diagonal(c):
        row = lax.broadcasted_iota(jnp.int32, (size_k, TILE), 0)
        col = lax.broadcasted_iota(jnp.int32, (size_k, TILE), 1) + c * TILE
        return row == col

    def gram_tile(c, square):
        at = columns(c)
        both = jnp.dot(left[...], flat[:, at], preferred_element_type=jnp.float32)
        system = jnp.where(diagonal(c), 1.0, 0.0) + both[:size_k] * (1.0 / (size_k - 1))
        held[:, at] = system
        drive[0:1, at] = both[size_k : size_k + 1] + both[size_k + 1 : size_k + 2]
        return square + jnp.sum(system * system, axis=0, keepdims=True)

    square = lax.fori_loop(0, tiles, gram_tile, jnp.zeros((1, TILE), jnp.float32))
    total = jnp.sum(square, axis=1, keepdims=True)
    norm_scale = 2.0 * jnp.sqrt(total / size_k + 1e-06)
    inv_norm = 1.0 / norm_scale
    inv_root = 1.0 / jnp.sqrt(norm_scale)

    @pl.loop(0, tiles)
    def _(c):
        at = columns(c)
        centred = held[:, at] * inv_norm - jnp.where(diagonal(c), 0.5, 0.0)
        held[:, at] = centred
        cb[:, at] = centred.astype(jnp.bfloat16)

    @pl.loop(0, tiles)
    def _(c):
        at = columns(c)
        second = jnp.dot(cb[...], cb[:, at], preferred_element_type=jnp.float32)
        first = held[:, at]
        xb[:, at] = second.astype(jnp.bfloat16)
        wb[:, at] = (POLY[4] * second + POLY[3] * first).astype(jnp.bfloat16)
        held[:, at] = jnp.where(diagonal(c), POLY[0], 0.0) + POLY[1] * first + POLY[2] * second

    def root_tile(c, acc):
        at = columns(c)
        high = jnp.dot(xb[...], wb[:, at], preferred_element_type=jnp.float32)
        root = (held[:, at] + high) * inv_root
        held[:, at] = root
        return acc + jnp.sum(root * drive[0:1, at], axis=1, keepdims=True)

    inner = lax.fori_loop(0, tiles, root_tile, jnp.zeros((size_k, 1), jnp.float32))

    @pl.loop(0, tiles)
    def _(c):
        at = columns(c)
        root = held[:, at]
        mean_weight = jnp.sum(root * inner, axis=0, keepdims=True) * (1.0 / (size_k - 1))
        out_ref[:, at] = (root + mean_weight).astype(jnp.bfloat16)


def three_weights(first, second, row_weight, extra, dev_rows):
    blocks, _, size_k = first.shape
    rows = blocks * dev_rows
    flops = 3 * 2 * size_k * size_k * (rows + 2 * size_k)
    return pl.pallas_call(
        weights_kernel,
        grid=(3,),
        out_shape=jax.ShapeDtypeStruct((size_k, 3 * size_k), jnp.bfloat16),
        in_specs=[
            pl.BlockSpec(first.shape, lambda t: (0, 0, 0), pipeline_mode=pl.Buffered(1)),
            pl.BlockSpec(second.shape, lambda t: (0, 0, 0), pipeline_mode=pl.Buffered(1)),
            pl.BlockSpec((1, 1, rows), lambda t: (t, 0, 0)),
            pl.BlockSpec((1, EXTRA, rows), lambda t: (t, 0, 0)),
        ],
        out_specs=pl.BlockSpec((size_k, size_k), lambda t: (0, t)),
        scratch_shapes=[
            pltpu.VMEM((rows, size_k), jnp.bfloat16),
            pltpu.VMEM((size_k, rows), jnp.bfloat16),
            pltpu.VMEM((size_k + EXTRA, rows), jnp.bfloat16),
            pltpu.VMEM((size_k, size_k), jnp.float32),
            pltpu.VMEM((size_k, size_k), jnp.bfloat16),
            pltpu.VMEM((size_k, size_k), jnp.bfloat16),
            pltpu.VMEM((size_k, size_k), jnp.bfloat16),
            pltpu.VMEM((8, size_k), jnp.float32),
        ],
        compiler_params=pltpu.CompilerParams(vmem_limit_bytes=VMEM_BYTES),
        cost_estimate=pl.CostEstimate(flops=flops, bytes_accessed=12 * 1024 * 1024, transcendentals=0),
    )(first, second, row_weight, extra)


def blend_kernel(member_ref, weight_ref, share_ref, out_ref, shared):
    values = member_ref[...].astype(jnp.float32)
    size_k = values.shape[0]
    mean_field = jnp.sum(values, axis=0, keepdims=True) / size_k
    anomaly = values - mean_field
    for t in range(3):
        shared[t * size_k : (t + 1) * size_k, :] = (anomaly * share_ref[t : t + 1, :]).astype(jnp.bfloat16)
    moved = jnp.dot(weight_ref[...], shared[...], preferred_element_type=jnp.float32)
    out_ref[...] = (moved + mean_field).astype(jnp.bfloat16)


def blend(by_column, weights, shares):
    size_k, width = by_column.shape
    return pl.pallas_call(
        blend_kernel,
        grid=(width // BLEND_TILE,),
        out_shape=jax.ShapeDtypeStruct(by_column.shape, jnp.bfloat16),
        in_specs=[
            pl.BlockSpec((size_k, BLEND_TILE), lambda c: (0, c)),
            pl.BlockSpec(weights.shape, lambda c: (0, 0), pipeline_mode=pl.Buffered(1)),
            pl.BlockSpec((3, BLEND_TILE), lambda c: (0, c)),
        ],
        out_specs=pl.BlockSpec((size_k, BLEND_TILE), lambda c: (0, c)),
        scratch_shapes=[pltpu.VMEM((3 * size_k, BLEND_TILE), jnp.bfloat16)],
        compiler_params=pltpu.CompilerParams(vmem_limit_bytes=VMEM_BYTES),
        cost_estimate=pl.CostEstimate(
            flops=6 * size_k * size_k * width, bytes_accessed=14 * 1024 * 1024, transcendentals=0
        ),
    )(by_column, weights, shares)


def split(values):
    high = lax.reduce_precision(values, 8, 7)
    low = lax.reduce_precision(values - high, 8, 7)
    return high.astype(jnp.bfloat16), low.astype(jnp.bfloat16)


def gather_kernel(half, src, dst, out_send, out_recv, pair_send, pair_recv, own):
    me = lax.axis_index("sub")
    core, chip = lax.rem(me, 2), me // 2
    partner = me + 1 - 2 * core

    def same(offset):
        return 2 * lax.rem(chip + offset, half) + core

    def remote(source, slot, send, recv, target):
        return pltpu.make_async_remote_copy(
            src_ref=source,
            dst_ref=dst.at[slot],
            send_sem=send,
            recv_sem=recv,
            device_id={"sub": target},
            device_id_type=pl.DeviceIdType.MESH,
        )

    barrier = pltpu.get_barrier_semaphore()
    for target in [partner] + [same(i) for i in range(1, half)]:
        pl.semaphore_signal(barrier, inc=1, device_id={"sub": target}, device_id_type=pl.DeviceIdType.MESH)
    pl.semaphore_wait(barrier, half)

    outward = []
    for i in range(1, half):
        outward.append(remote(src, me, out_send.at[i], out_recv.at[i], same(i)))
        outward[-1].start()
    across = [remote(src, me, pair_send.at[0], pair_recv.at[0], partner)]
    across[0].start()
    kept = pltpu.make_async_copy(src, dst.at[me], own)
    kept.start()
    for i in range(1, half):
        outward[i - 1].wait_recv()
        owner = same(half - i)
        across.append(remote(dst.at[owner], owner, pair_send.at[i], pair_recv.at[i], partner))
        across[-1].start()
    kept.wait()
    for copy in outward:
        copy.wait_send()
    for copy in across:
        copy.wait()


def gather_rows(packed, number):
    size = lax.axis_size("sub")
    half = size // 2
    return pl.pallas_call(
        functools.partial(gather_kernel, half),
        out_shape=jax.ShapeDtypeStruct((size,) + packed.shape, packed.dtype),
        in_specs=[pl.BlockSpec(memory_space=pl.ANY)],
        out_specs=pl.BlockSpec(memory_space=pl.ANY),
        scratch_shapes=[pltpu.SemaphoreType.DMA((half,))] * 4 + [pltpu.SemaphoreType.DMA],
        compiler_params=pltpu.CompilerParams(collective_id=number, has_side_effects=True),
        cost_estimate=pl.CostEstimate(flops=0, bytes_accessed=64 * 1024 * 1024, transcendentals=0),
    )(packed)


def local(
    members,
    obs_perturb,
    innovations,
    obs_list,
    obs_blocks,
    obs_precision,
    interp_slots,
    interp_weight,
):
    n_sub = lax.axis_size("sub")
    me = lax.axis_index("sub")
    dev_rows, size_k = obs_perturb.shape
    rows = n_sub * dev_rows
    inside = jnp.arange(obs_list.shape[1], dtype=jnp.int32) < obs_blocks[0] * BLOCK
    rho = jnp.where(inside, obs_precision[0], jnp.float32(0.0))
    high, low = split(rows_weight(obs_list[0], rho, rows))
    tail = jnp.concatenate([high, low, innovations])
    tail = jnp.pad(tail, (0, EXTRA * size_k - tail.shape[0])).reshape(EXTRA, size_k)
    half_rows = dev_rows // 2
    first = gather_rows(obs_perturb[:half_rows], 0)
    packed = jnp.concatenate([obs_perturb[half_rows:], tail], axis=0)
    members, packed, first = lax.optimization_barrier((members, packed, first))
    by_column = lax.all_to_all(members, ("region", "sub"), split_axis=1, concat_axis=0, tiled=True)

    second = gather_rows(packed, 1)
    tails = second[:, half_rows:, :].reshape(n_sub, EXTRA * size_k)
    innov = tails[:, 2 * rows : 2 * rows + dev_rows].reshape(rows).astype(jnp.float32)
    near = jnp.stack(
        [lax.dynamic_index_in_dim(tails, lax.rem(me + s, n_sub), 0, False) for s in (n_sub - 1, 0, 1)]
    ).astype(jnp.float32)
    weight = near[:, :rows] + near[:, rows : 2 * rows]
    extra = jnp.stack(split(weight * innov[None, :]), axis=1)
    extra = jnp.pad(extra, ((0, 0), (0, EXTRA - 2), (0, 0)))
    weights = three_weights(first, second, weight[:, None, :], extra, dev_rows)

    slots = jnp.arange(3, dtype=jnp.int32)[:, None]
    share = jnp.where(interp_slots[None, :, 0] == slots, interp_weight[None], 0.0) + jnp.where(
        interp_slots[None, :, 1] == slots, 1.0 - interp_weight[None], 0.0
    )
    return blend(by_column, weights, jnp.repeat(share, LEV * VARS, axis=1))


def solution(mesh):
    in_specs = (
        P(("region", "sub"), None),
        P(("region", "sub"), None),
        P(("region", "sub")),
        P(("region", "sub"), None),
        P(("region", "sub")),
        P(("region", "sub"), None),
        P(("region", "sub"), None),
        P(("region", "sub")),
    )
    out_specs = P(None, ("region", "sub"))
    return jax.shard_map(local, mesh=mesh, in_specs=in_specs, out_specs=out_specs, check_vma=False)
```
